32 devices in a mesh: node: 8 (over z, y), ctr: 4 (over x, core).
Axes of the slice: x: 2, y: 2, z: 4, core: 2. Of those that a mesh axis runs over, the one named last changes fastest.
Arguments:
- surface_xyz: float32 [3, 65536], P(None, ('node', 'ctr')), may hold values from 0 to 1
- centre_idx: int32 [32768], P(('node', 'ctr')), may hold values from 0 to 65535, as said below
- volume_xyz: float32 [3, 32768], P(None, 'node'), may hold values from 0 to 1
- slab_ids: int32 [32768], P('node'), may hold values from 0 to 32767, as said below
- cotangent: float32 [12, 32768], P(None, 'node'), may hold values from -6 to 6
Outputs:
- coef_adjoint: float32 [12, 32768], P(None, ('node', 'ctr'))
- residual: float32 [12, 32768], P(None, ('node', 'ctr'))
The draws below stay inside these ranges and needn't reach their ends.
Inputs may be any that keep to these rules, and one draw needn't show every extreme that they name: `centre_idx`: all entries are distinct, and 0 and 65535 are always among them. `slab_ids`: within each aligned block of 4096 entries (the nodes of one index of node) the entries are the ids of that same block, each once.
All inputs are finite; a program needn't handle non-finite values.
Results may differ from the reference program's by a relative error of at most 0.0003.
Values sent between devices are 32-bit elements; how exact they have to be, the bound alone decides.
A program may use at most 320 MiB of HBM per device.

```python
import math
import jax
import jax.numpy as jnp
from jax import lax

C = 32768
RHS = 12
ND = 4096
ITERS = 2
NODES = 32768
SURF = 65536


def draw_centre_idx(key, part):
    first_key, second_key = jax.random.split(key)
    inner = 1 + jax.random.permutation(first_key, SURF - 2)[:C - 2].astype(jnp.int32)
    chosen = jnp.concatenate([jnp.array([0, SURF - 1], jnp.int32), inner])
    return jax.random.permutation(second_key, chosen).astype(jnp.int32)


def draw_slab_ids(key, part):
    blocks = NODES // ND
    keys = jax.random.split(key, blocks)

    def block_order(block_key):
        return jax.random.permutation(block_key, ND).astype(jnp.int32)
    orders = jax.vmap(block_order)(keys)
    offsets = (jnp.arange(blocks, dtype=jnp.int32) * ND)[:, None]
    return (orders + offsets).reshape(-1).astype(jnp.int32)


def block_levels(key, shape, cuts, smallest, top_value):
    loudness, own = 1.0, jax.random.fold_in(key, 6)
    for axis_at, shards_of in cuts:
        draws = jnp.exp(jax.random.uniform(jax.random.fold_in(own, axis_at), (shards_of,), jnp.float32, smallest / len(cuts), top_value / len(cuts)))
        loudness = loudness * jnp.repeat(draws, shape[axis_at] // shards_of).reshape([-1 if axis == axis_at else 1 for axis in range(len(shape))])
    return loudness


def bell_draw(stream_key, extent, scale, bound, shards=(), kind=jnp.bfloat16):
    values = scale * jax.random.normal(stream_key, extent, jnp.float32)
    if shards:
        values = values * block_levels(stream_key, extent, shards, -0.22, 0.18)
    return jnp.clip(values, -bound, bound).astype(kind)


def setup_inputs(seed: int = 0) -> dict:
    streams_of = jax.random.split(jax.random.key(seed), 6)
    surface_xyz = jnp.clip(1.0 * jax.random.uniform(streams_of[0], (3, SURF), jnp.float32) ** block_levels(streams_of[0], (3, SURF), ((1, 32),), -0.2, 0.2), 0.0, 1.0)
    centre_idx = draw_centre_idx(jax.random.fold_in(streams_of[5], 71), 0)
    volume_xyz = jnp.clip(1.0 * jax.random.uniform(streams_of[2], (3, NODES), jnp.float32) ** block_levels(streams_of[2], (3, NODES), ((1, 8),), -0.2, 0.2), 0.0, 1.0)
    slab_ids = draw_slab_ids(jax.random.fold_in(streams_of[5], 71), 0)
    cotangent = bell_draw(streams_of[4], (RHS, NODES), 1.0, 6.0, ((1, 8),), jnp.float32)
    return {"surface_xyz": surface_xyz, "centre_idx": centre_idx, "volume_xyz": volume_xyz, "slab_ids": slab_ids, "cotangent": cotangent}


def support_radius(count):
    return 0.2

def kernel_apply(row_xyz, col_xyz, vectors, radius, tile_entries):
    rows = row_xyz.shape[1]
    cols = col_xyz.shape[1]
    row_step = math.gcd(rows, 2048)
    col_step = math.gcd(cols, max(1, tile_entries // row_step))
    blocks = row_xyz.reshape(3, rows // row_step, row_step).transpose(1, 0, 2)
    width = vectors.shape[0]

    def one_block(block_xyz):

        def add_tile(index, acc):
            tile_xyz = lax.dynamic_slice_in_dim(col_xyz, index * col_step, col_step, 1)
            tile_vec = lax.dynamic_slice_in_dim(vectors, index * col_step, col_step, 1)
            diff_x = block_xyz[0][:, None] - tile_xyz[0][None, :]
            diff_y = block_xyz[1][:, None] - tile_xyz[1][None, :]
            diff_z = block_xyz[2][:, None] - tile_xyz[2][None, :]
            dist_sq = diff_x * diff_x + diff_y * diff_y + diff_z * diff_z
            scaled = jnp.sqrt(dist_sq) / radius
            weight = jnp.maximum(1.0 - scaled, 0.0)
            weight_sq = weight * weight
            kernel = weight_sq * weight_sq * (4.0 * scaled + 1.0)
            return acc + lax.dot_general(tile_vec, kernel, (((1,), (1,)), ((), ())), precision=lax.Precision.HIGHEST, preferred_element_type=jnp.float32)
        return lax.fori_loop(0, cols // col_step, add_tile, jnp.zeros((width, row_step), jnp.float32))
    result = lax.map(one_block, blocks)
    return result.transpose(1, 0, 2).reshape(width, rows)

def reference(surface_xyz, centre_idx, volume_xyz, slab_ids, cotangent):
    centres = jnp.take(surface_xyz, centre_idx, axis=1)
    nodes = jnp.take(volume_xyz, slab_ids, axis=1)
    radius = support_radius(centres.shape[1])
    pulled = kernel_apply(centres, nodes, cotangent, radius, 1 << 22)
    solution = jnp.zeros_like(pulled)
    resid = pulled
    direction = pulled
    norm_now = lax.optimization_barrier(jnp.sum(resid * resid, axis=1))
    for step in range(ITERS):
        image = kernel_apply(centres, centres, direction, radius, 1 << 22)
        step_len = norm_now / lax.optimization_barrier(jnp.sum(direction * image, axis=1))
        solution = solution + step_len[:, None] * direction
        resid = resid - step_len[:, None] * image
        norm_next = lax.optimization_barrier(jnp.sum(resid * resid, axis=1))
        direction = resid + (norm_next / norm_now)[:, None] * direction
        norm_now = norm_next
    return (solution, resid)
```

```python
import functools
import math

import jax
import jax.numpy as jnp
from jax import lax
from jax.experimental import pallas as pl
from jax.experimental.pallas import tpu as pltpu
from jax.sharding import PartitionSpec as P

RADIUS = 0.2
LANES = 128
PAD = 16
VMEM = 50 * 1024 * 1024
NT = (((1,), (1,)), ((), ()))


def split3(value):
    first = lax.reduce_precision(value, 8, 7)
    rest = value - first
    second = lax.reduce_precision(rest, 8, 7)
    return first, second, lax.reduce_precision(rest - second, 8, 7)


def lookup(table, ids):
    rows = table.shape[1] // LANES
    parts = jnp.concatenate([part.reshape(3, rows, LANES) for part in split3(table)], axis=0)
    parts = parts.transpose(1, 0, 2).reshape(rows, 9 * LANES).astype(jnp.bfloat16)
    high = (ids[:, None] // LANES == jnp.arange(rows, dtype=jnp.int32)[None, :]).astype(jnp.bfloat16)
    picked = jnp.dot(high, parts, preferred_element_type=jnp.float32)
    low = ids[:, None] % LANES == jnp.arange(LANES, dtype=jnp.int32)[None, :]
    picked = picked.reshape(-1, 9, LANES)
    picked = jnp.sum(jnp.where(low[:, None, :], picked, 0.0), axis=2)
    return (picked[:, 0:3] + picked[:, 3:6] + picked[:, 6:9]).T


def column_features(xyz):
    point = (xyz - 0.5) * (1.0 / RADIUS)
    square = jnp.sum(point * point, axis=0, keepdims=True)
    one = jnp.ones_like(square)
    return jnp.concatenate([point, square, one, jnp.zeros((3, xyz.shape[1]), jnp.float32)], axis=0)


def row_features(column):
    zero = jnp.zeros_like(column[5:8])
    alpha = jnp.concatenate([-2.0 * column[0:3], column[4:5], column[3:4], zero], axis=0)
    a1, a2, a3 = split3(alpha)
    return jnp.concatenate([a1, a1, a2, a2, a1, a3], axis=0).T.astype(jnp.bfloat16)


def rounded(value):
    return value.astype(jnp.bfloat16).astype(jnp.float32)


def right_factor(beta):
    b1 = rounded(beta)
    rest = beta - b1
    b2 = rounded(rest)
    b3 = rest - b2
    return jnp.concatenate([b1, b2, b1, b2, b3, b1], axis=0).astype(jnp.bfloat16)


def two_parts(vectors):
    v1 = rounded(vectors)
    return jnp.concatenate([v1, vectors - v1], axis=0).astype(jnp.bfloat16)


def finish(acc, out_ref):
    total = acc[...].T
    out_ref[...] = 4.0 * (total[:PAD] + total[PAD:])


def apply_body(row_tile, keep, left_ref, beta_ref, vec_ref, out_ref, *rest):
    if keep:
        hi_ref, lo_ref, acc = rest
    else:
        (acc,) = rest
    rows = left_ref.shape[0]
    step = pl.program_id(0)

    @pl.when(step == 0)
    def _():
        acc[...] = jnp.zeros_like(acc)

    right = right_factor(beta_ref[0])
    vec = two_parts(vec_ref[0])

    for index in range(rows // row_tile):
        here = pl.ds(index * row_tile, row_tile)
        q = jnp.dot(left_ref[here, :], right, preferred_element_type=jnp.float32)
        q = jnp.minimum(jnp.maximum(q, 1e-30), 1.0)
        s = q * lax.rsqrt(q)
        w = 1.0 - s
        w2 = w * w
        k = (w2 * w2) * (0.25 + s)
        hi = k.astype(jnp.bfloat16)
        lo = (k - hi.astype(jnp.float32)).astype(jnp.bfloat16)
        if keep:
            hi_ref[here, :] = hi
            lo_ref[here, :] = lo
        acc[here, :] += lax.dot_general(
            hi, vec, NT, preferred_element_type=jnp.float32
        ) + lax.dot_general(lo, vec, NT, preferred_element_type=jnp.float32)

    @pl.when(step == pl.num_programs(0) - 1)
    def _():
        finish(acc, out_ref)


def stored_body(row_tile, hi_ref, lo_ref, vec_ref, out_ref, acc):
    rows = hi_ref.shape[0]
    step = pl.program_id(0)

    @pl.when(step == 0)
    def _():
        acc[...] = jnp.zeros_like(acc)

    vec = two_parts(vec_ref[0])
    for index in range(rows // row_tile):
        here = pl.ds(index * row_tile, row_tile)
        acc[here, :] += lax.dot_general(
            hi_ref[here, :], vec, NT, preferred_element_type=jnp.float32
        ) + lax.dot_general(lo_ref[here, :], vec, NT, preferred_element_type=jnp.float32)

    @pl.when(step == pl.num_programs(0) - 1)
    def _():
        finish(acc, out_ref)


def apply_kernel(left, beta, vec, beta_row, vec_row, block, keep):
    rows = left.shape[0]
    chunks, _, chunk = beta.shape
    per = chunk // block
    steps = chunks * per
    row_tile = math.gcd(rows, 256)
    out_shape = [jax.ShapeDtypeStruct((PAD, rows), jnp.float32)]
    out_specs = [pl.BlockSpec((PAD, rows), lambda j: (0, 0))]
    if keep:
        out_shape += [jax.ShapeDtypeStruct((rows, chunks * chunk), jnp.bfloat16)] * 2
        out_specs += [pl.BlockSpec((rows, block), lambda j: (0, j))] * 2
    return pl.pallas_call(
        functools.partial(apply_body, row_tile, keep),
        grid=(steps,),
        in_specs=[
            pl.BlockSpec(left.shape, lambda j: (0, 0)),
            pl.BlockSpec((1, 8, block), lambda j: (j // per, beta_row, j % per)),
            pl.BlockSpec((1, PAD, block), lambda j: (j // per, vec_row, j % per)),
        ],
        out_shape=out_shape,
        out_specs=out_specs,
        scratch_shapes=[pltpu.VMEM((rows, 2 * PAD), jnp.float32)],
        compiler_params=pltpu.CompilerParams(vmem_limit_bytes=VMEM),
        cost_estimate=pl.CostEstimate(
            flops=rows * chunks * chunk * 400, bytes_accessed=1 << 20, transcendentals=0
        ),
    )(left, beta, vec)


def apply_stored(hi, lo, vec):
    rows = hi.shape[0]
    chunks, _, chunk = vec.shape
    row_tile = math.gcd(rows, 256)
    return pl.pallas_call(
        functools.partial(stored_body, row_tile),
        grid=(chunks,),
        in_specs=[
            pl.BlockSpec((rows, chunk), lambda j: (0, j)),
            pl.BlockSpec((rows, chunk), lambda j: (0, j)),
            pl.BlockSpec((1, PAD, chunk), lambda j: (j, 0, 0)),
        ],
        out_shape=jax.ShapeDtypeStruct((PAD, rows), jnp.float32),
        out_specs=pl.BlockSpec((PAD, rows), lambda j: (0, 0)),
        scratch_shapes=[pltpu.VMEM((rows, 2 * PAD), jnp.float32)],
        compiler_params=pltpu.CompilerParams(vmem_limit_bytes=VMEM),
        cost_estimate=pl.CostEstimate(
            flops=rows * chunks * chunk * 128, bytes_accessed=hi.size * 4, transcendentals=0
        ),
    )(hi, lo, vec)


def local(surface_xyz, centre_idx, volume_xyz, slab_ids, cotangent):
    everyone = ("node", "ctr")
    width = cotangent.shape[0]
    surface = lax.all_gather(surface_xyz.reshape(-1), everyone, axis=0)
    devices = surface.shape[0]
    surface = surface.reshape(devices, 3, -1).transpose(1, 0, 2).reshape(3, -1)

    nodes = lookup(volume_xyz, slab_ids % volume_xyz.shape[1])
    zeros = jnp.zeros((PAD - width, cotangent.shape[1]), jnp.float32)
    packed = jnp.concatenate([cotangent, zeros, column_features(nodes)], axis=0)
    packed = lax.all_gather(packed, "node", axis=0)

    mine = column_features(lookup(surface, centre_idx))
    left = row_features(mine)
    beta = lax.all_gather(mine, everyone, axis=0)
    owned = mine.shape[1]

    block = math.gcd(packed.shape[2], 1024)
    pulled = apply_kernel(left, packed, packed, PAD // 8, 0, block, False)[0]
    pulled_all = lax.all_gather(pulled, everyone, axis=0)
    image, hi, lo = apply_kernel(left, beta, pulled_all, 0, 0, owned, True)
    image_all = lax.all_gather(image, everyone, axis=0)

    real = jnp.arange(PAD) < width

    def safe(value):
        return jnp.where(real, value, 1.0)

    norm = safe(jnp.sum(pulled_all * pulled_all, axis=(0, 2)))
    step_len = norm / safe(jnp.sum(pulled_all * image_all, axis=(0, 2)))
    resid_all = pulled_all - step_len[:, None] * image_all
    norm_next = jnp.sum(resid_all * resid_all, axis=(0, 2))
    ratio = norm_next / norm
    direction_all = resid_all + ratio[:, None] * pulled_all
    solution_mine = step_len[:, None] * pulled
    resid = pulled - step_len[:, None] * image
    direction = resid + ratio[:, None] * pulled

    image = apply_stored(hi, lo, direction_all)
    curve = lax.psum(jnp.sum(direction * image, axis=1), everyone)
    step_len = (norm_next / safe(curve))[:, None]
    solution_mine = solution_mine + step_len * direction
    resid = resid - step_len * image
    return (solution_mine[:width], resid[:width])


def solution(mesh):
    return jax.shard_map(
        local,
        mesh=mesh,
        in_specs=(
            P(None, ("node", "ctr")),
            P(("node", "ctr")),
            P(None, "node"),
            P("node"),
            P(None, "node"),
        ),
        out_specs=(P(None, ("node", "ctr")), P(None, ("node", "ctr"))),
        check_vma=False,
    )
```

```python
import functools
import math

import jax
import jax.numpy as jnp
from jax import lax
from jax.experimental import pallas as pl
from jax.experimental.pallas import tpu as pltpu
from jax.sharding import PartitionSpec as P

RADIUS = 0.2
LANES = 128
PAD = 16
VMEM = 50 * 1024 * 1024
NT = (((1,), (1,)), ((), ()))


def split3(value):
    first = lax.reduce_precision(value, 8, 7)
    rest = value - first
    second = lax.reduce_precision(rest, 8, 7)
    return first, second, lax.reduce_precision(rest - second, 8, 7)


def lookup(table, ids):
    rows = table.shape[1] // LANES
    parts = jnp.concatenate([part.reshape(3, rows, LANES) for part in split3(table)], axis=0)
    parts = parts.transpose(1, 0, 2).reshape(rows, 9 * LANES).astype(jnp.bfloat16)
    high = (ids[:, None] // LANES == jnp.arange(rows, dtype=jnp.int32)[None, :]).astype(jnp.bfloat16)
    picked = jnp.dot(high, parts, preferred_element_type=jnp.float32)
    low = ids[:, None] % LANES == jnp.arange(LANES, dtype=jnp.int32)[None, :]
    picked = picked.reshape(-1, 9, LANES)
    picked = jnp.sum(jnp.where(low[:, None, :], picked, 0.0), axis=2)
    return (picked[:, 0:3] + picked[:, 3:6] + picked[:, 6:9]).T


def scaled(xyz):
    point = (xyz - 0.5) * (1.0 / RADIUS)
    return jnp.concatenate([point, jnp.ones((1, xyz.shape[1]), jnp.float32)], axis=0)


def row_features(point):
    square = jnp.sum(point[:3] * point[:3], axis=0, keepdims=True)
    alpha = jnp.concatenate(
        [jnp.ones_like(square), jnp.zeros_like(point[:3]), -2.0 * point[:3], square], axis=0
    )
    a1, a2, a3 = split3(alpha)
    return jnp.concatenate([a1, a1, a2, a2, a1, a3], axis=0).T.astype(jnp.bfloat16)


def rounded(value):
    return value.astype(jnp.bfloat16).astype(jnp.float32)


def right_factor(group):
    row = lax.broadcasted_iota(jnp.int32, group.shape, 0)
    place = jnp.where(row >= 4, group, 0.0)
    square = jnp.sum(jnp.where(row < 7, place * place, 0.0), axis=0, keepdims=True)
    beta = jnp.where(row == 0, square, place)
    b1 = rounded(beta)
    rest = beta - b1
    b2 = rounded(rest)
    b3 = rest - b2
    return jnp.concatenate([b1, b2, b1, b2, b3, b1], axis=0).astype(jnp.bfloat16)


def two_parts(vectors):
    v1 = rounded(vectors)
    return jnp.concatenate([v1, vectors - v1], axis=0).astype(jnp.bfloat16)


def finish(acc, out_ref):
    total = acc[...].T
    out_ref[...] = 4.0 * (total[:PAD] + total[PAD:])


def side_by_side(make, ref):
    return jnp.concatenate([make(ref[index]) for index in range(ref.shape[0])], axis=1)


def apply_body(row_tile, keep, left_ref, beta_ref, vec_ref, out_ref, *rest):
    if keep:
        hi_ref, lo_ref, acc = rest
    else:
        (acc,) = rest
    rows = left_ref.shape[0]
    step = pl.program_id(0)

    @pl.when(step == 0)
    def _():
        acc[...] = jnp.zeros_like(acc)

    right = side_by_side(right_factor, beta_ref)
    vec = side_by_side(two_parts, vec_ref)
    vec = jnp.concatenate([vec, vec], axis=1)

    for index in range(rows // row_tile):
        here = pl.ds(index * row_tile, row_tile)
        q = jnp.dot(left_ref[here, :], right, preferred_element_type=jnp.float32)
        q = jnp.minimum(jnp.maximum(q, 1e-30), 1.0)
        s = q * lax.rsqrt(q)
        w = 1.0 - s
        w2 = w * w
        k = (w2 * w2) * (0.25 + s)
        hi = k.astype(jnp.bfloat16)
        lo = (k - hi.astype(jnp.float32)).astype(jnp.bfloat16)
        if keep:
            hi_ref[here, :] = hi
            lo_ref[here, :] = lo
        acc[here, :] += lax.dot_general(
            jnp.concatenate([hi, lo], axis=1), vec, NT, preferred_element_type=jnp.float32
        )

    @pl.when(step == pl.num_programs(0) - 1)
    def _():
        finish(acc, out_ref)


def stored_body(hi_ref, lo_ref, vec_ref, out_ref, acc):
    step = pl.program_id(0)

    @pl.when(step == 0)
    def _():
        acc[...] = jnp.zeros_like(acc)

    vec = side_by_side(two_parts, vec_ref)
    acc[...] += lax.dot_general(
        hi_ref[...], vec, NT, preferred_element_type=jnp.float32
    ) + lax.dot_general(lo_ref[...], vec, NT, preferred_element_type=jnp.float32)

    @pl.when(step == pl.num_programs(0) - 1)
    def _():
        finish(acc, out_ref)


def apply_kernel(left, beta, vec, beta_block, vec_block, beta_map, vec_map, steps, keep):
    rows = left.shape[0]
    block = beta_block[0] * beta_block[2]
    row_tile = math.gcd(rows, 256)
    out_shape = [jax.ShapeDtypeStruct((PAD, rows), jnp.float32)]
    out_specs = [pl.BlockSpec((PAD, rows), lambda j: (0, 0))]
    if keep:
        out_shape += [jax.ShapeDtypeStruct((rows, steps * block), jnp.bfloat16)] * 2
        out_specs += [pl.BlockSpec((rows, block), lambda j: (0, j))] * 2
    return pl.pallas_call(
        functools.partial(apply_body, row_tile, keep),
        grid=(steps,),
        in_specs=[
            pl.BlockSpec(left.shape, lambda j: (0, 0)),
            pl.BlockSpec(beta_block, beta_map),
            pl.BlockSpec(vec_block, vec_map),
        ],
        out_shape=out_shape,
        out_specs=out_specs,
        scratch_shapes=[pltpu.VMEM((rows, 2 * PAD), jnp.float32)],
        compiler_params=pltpu.CompilerParams(vmem_limit_bytes=VMEM),
        cost_estimate=pl.CostEstimate(
            flops=rows * steps * block * 3000, bytes_accessed=1 << 20, transcendentals=0
        ),
    )(left, beta, vec)


def apply_stored(hi, lo, vec):
    rows = hi.shape[0]
    chunks, _, chunk = vec.shape
    group = math.gcd(chunks, max(1, 1024 // chunk))
    block = group * chunk
    return pl.pallas_call(
        stored_body,
        grid=(chunks // group,),
        in_specs=[
            pl.BlockSpec((rows, block), lambda j: (0, j)),
            pl.BlockSpec((rows, block), lambda j: (0, j)),
            pl.BlockSpec((group, PAD, chunk), lambda j: (j, 0, 0)),
        ],
        out_shape=jax.ShapeDtypeStruct((PAD, rows), jnp.float32),
        out_specs=pl.BlockSpec((PAD, rows), lambda j: (0, 0)),
        scratch_shapes=[pltpu.VMEM((rows, 2 * PAD), jnp.float32)],
        compiler_params=pltpu.CompilerParams(vmem_limit_bytes=VMEM),
        cost_estimate=pl.CostEstimate(
            flops=rows * chunks * chunk * 128, bytes_accessed=hi.size * 4, transcendentals=0
        ),
    )(hi, lo, vec)


def local(surface_xyz, centre_idx, volume_xyz, slab_ids, cotangent):
    everyone = ("node", "ctr")
    width = cotangent.shape[0]
    surface = lax.all_gather(surface_xyz.reshape(-1), everyone, axis=0)
    devices = surface.shape[0]
    surface = surface.reshape(devices, 3, -1).transpose(1, 0, 2).reshape(3, -1)

    nodes = lookup(volume_xyz, slab_ids % volume_xyz.shape[1])
    packed = jnp.concatenate([cotangent, scaled(nodes)], axis=0)
    packed = lax.all_gather(packed, "node", axis=0)

    mine = scaled(lookup(surface, centre_idx))
    left = row_features(mine)
    beta = lax.all_gather(jnp.concatenate([jnp.zeros_like(mine), mine], axis=0), everyone, axis=0)
    owned = mine.shape[1]
    half = owned // 2

    block = math.gcd(packed.shape[2], 1024)
    per = packed.shape[2] // block
    group = math.gcd(devices, max(1, 1024 // half))
    pulled_parts, gathered = [], []
    for part in range(2):
        pulled = apply_kernel(
            left[part * half : (part + 1) * half],
            packed,
            packed,
            (1, 8, block),
            (1, PAD, block),
            lambda j: (j // per, 1, j % per),
            lambda j: (j // per, 0, j % per),
            per * packed.shape[0],
            False,
        )[0]
        pulled_parts.append(pulled)
        gathered.append(lax.all_gather(pulled, everyone, axis=0))
    pulled = jnp.concatenate(pulled_parts, axis=1)
    pulled_all = jnp.concatenate(gathered, axis=2)

    image = 0.0
    kept = []
    for part in range(2):
        term, hi, lo = apply_kernel(
            left,
            beta,
            gathered[part],
            (group, 8, half),
            (group, PAD, half),
            lambda j, part=part: (j, 0, part),
            lambda j: (j, 0, 0),
            devices // group,
            True,
        )
        image = image + term
        kept.append((hi, lo))
    image_all = lax.all_gather(image, everyone, axis=0)

    real = jnp.arange(PAD) < width

    def safe(value):
        return jnp.where(real, value, 1.0)

    norm = safe(jnp.sum(pulled_all * pulled_all, axis=(0, 2)))
    step_len = norm / safe(jnp.sum(pulled_all * image_all, axis=(0, 2)))
    resid_all = pulled_all - step_len[:, None] * image_all
    norm_next = jnp.sum(resid_all * resid_all, axis=(0, 2))
    ratio = norm_next / norm
    direction_all = resid_all + ratio[:, None] * pulled_all
    solution_mine = step_len[:, None] * pulled
    resid = pulled - step_len[:, None] * image
    direction = resid + ratio[:, None] * pulled

    image = apply_stored(*kept[0], direction_all[:, :, :half]) + apply_stored(
        *kept[1], direction_all[:, :, half:]
    )
    curve = lax.psum(jnp.sum(direction * image, axis=1), everyone)
    step_len = (norm_next / safe(curve))[:, None]
    solution_mine = solution_mine + step_len * direction
    resid = resid - step_len * image
    return (solution_mine[:width], resid[:width])


def solution(mesh):
    return jax.shard_map(
        local,
        mesh=mesh,
        in_specs=(
            P(None, ("node", "ctr")),
            P(("node", "ctr")),
            P(None, "node"),
            P("node"),
            P(None, "node"),
        ),
        out_specs=(P(None, ("node", "ctr")), P(None, ("node", "ctr"))),
        check_vma=False,
    )
```
